32 devices in a mesh: dp: 4 (over x, core), ens: 8 (over z, y).
Axes of the slice: x: 2, y: 2, z: 4, core: 2. Of those that a mesh axis runs over, the one named last changes fastest.
Arguments:
- embed: bfloat16 [4, 128, 128, 256], P('dp', 'ens'), may hold values from -6 to 6
- counts: int32 [4, 128], P('dp', 'ens'), may hold values from 4 to 128, as said below
- member: int32 [4, 128], P('dp', 'ens'), may hold values from 0 to 3, as said below
- bins: int32 [4, 128, 128, 128], P('dp', 'ens'), may hold values from 0 to 7
- masses: float32 [4, 4], P('dp'), may hold values from -1.5 to 1.5
- gain_attn: float32 [1, 256], replicated, may hold values from 0.25 to 1.75
- w_qkv: bfloat16 [1, 256, 768], replicated, may hold values from -0.375 to 0.375
- w_out: bfloat16 [1, 256, 256], replicated, may hold values from -0.375 to 0.375
- pair_table: float32 [1, 8, 8], replicated, may hold values from -4 to 4
- gain_ffn: float32 [1, 256], replicated, may hold values from 0.25 to 1.75
- w_up: bfloat16 [1, 256, 1024], replicated, may hold values from -0.375 to 0.375
- w_down: bfloat16 [1, 1024, 256], replicated, may hold values from -0.1875 to 0.1875
- w_phi: bfloat16 [256, 256], replicated, may hold values from -0.375 to 0.375
- w_mean: float32 [256], replicated, may hold values from -0.375 to 0.375
- w_scale: float32 [256], replicated, may hold values from -0.375 to 0.375
Outputs:
- neg_loglik: float32 [4, 4], P('dp')
- grad_gain_attn: float32 [1, 256], replicated
- grad_w_qkv: float32 [1, 256, 768], replicated
- grad_w_out: float32 [1, 256, 256], replicated
- grad_pair_table: float32 [1, 8, 8], replicated
- grad_gain_ffn: float32 [1, 256], replicated
- grad_w_up: float32 [1, 256, 1024], replicated
- grad_w_down: float32 [1, 1024, 256], replicated
- grad_w_phi: float32 [256, 256], replicated
- grad_w_mean: float32 [256], replicated
- grad_w_scale: float32 [256], replicated
The draws below stay inside these ranges and needn't reach their ends.
Inputs may be any that keep to these rules, and one draw needn't show every extreme that they name: `counts`: every run of 16 consecutive jets of a group holds a jet with 128 constituents. `member`: every run of 16 consecutive jets of a group holds at least one jet of each ensemble.
All inputs are finite; a program needn't handle non-finite values.
Results may differ from the reference program's by a relative error of at most 0.028.
Values sent between devices are 32-bit elements; how exact they have to be, the bound alone decides.
A program may use at most 128 MiB of HBM per device.

```python
import math
import jax
import jax.numpy as jnp
from jax import lax

D = 256
H = 8
FF = 1024
NC = 128
NBIN = 8
DP = 256
GE = 4
LAYERS = 1
JET_DEV = 16
JETS = 128
N_DP = 4
N_ENS = 8


def draw_counts(key, part):
    raw = jax.random.randint(key, (N_DP, JETS), 4, NC + 1, dtype=jnp.int32)
    position = jnp.arange(JETS, dtype=jnp.int32) % JET_DEV
    return jnp.where(position[None, :] == 0, NC, raw).astype(jnp.int32)


def draw_member(key, part):
    raw = jax.random.randint(jax.random.fold_in(key, 7), (N_DP, N_ENS, JET_DEV), 0, GE, dtype=jnp.int32)
    scores = jax.random.randint(jax.random.fold_in(key, 11), (N_DP, N_ENS, GE), 0, 1 << 20, dtype=jnp.int32)
    scores = scores * GE + jnp.arange(GE, dtype=jnp.int32)
    firsts = jnp.argsort(scores, axis=-1, stable=True).astype(jnp.int32)
    merged = jnp.concatenate([firsts, raw[..., GE:]], axis=-1)
    return merged.reshape(N_DP, JETS).astype(jnp.int32)


def set_ends(values, key, low, top_value):
    index_at = [jax.random.randint(jax.random.fold_in(key, axis), (), 0, length) for axis, length in enumerate(values.shape)]
    longest = values.shape.index(max(values.shape))
    neighbour = index_at[:longest] + [(index_at[longest] + 1) % values.shape[longest]] + index_at[longest + 1:]
    return values.at[tuple(index_at)].set(low).at[tuple(neighbour)].set(top_value)


def shard_levels(own_key, shape, split, smallest, largest):
    def one(dim, parts):
        heights = jax.random.uniform(jax.random.fold_in(jax.random.fold_in(own_key, 6), dim), (parts,), jnp.float32, smallest / len(split), largest / len(split))
        return jnp.repeat(jnp.exp(heights), shape[dim] // parts).reshape((-1,) + (1,) * (len(shape) - dim - 1))

    factor_of = one(*split[0])
    for cut in split[1:]:
        factor_of = factor_of * one(*cut)
    return factor_of


def gaussian(key, extent, spread, most, split=(), kind=jnp.bfloat16):
    level = shard_levels(key, extent, split, -0.22, 0.18) if split else 1.0
    result = jax.random.normal(key, extent, jnp.float32) * spread * level
    return jnp.minimum(jnp.maximum(result, -most), most).astype(kind)


def setup_inputs(seed: int = 0) -> dict:
    arg_keys = jax.random.split(jax.random.key(seed), 16)
    return {
        "embed": gaussian(arg_keys[0], (N_DP, JETS, NC, D), 1.0, 6.0, ((0, 4), (1, 8))),
        "counts": draw_counts(jax.random.fold_in(arg_keys[15], 71), 0),
        "member": draw_member(jax.random.fold_in(arg_keys[15], 71), 0),
        "bins": set_ends(jax.random.randint(arg_keys[3], (N_DP, JETS, NC, NC), 0, NBIN), jax.random.fold_in(arg_keys[3], 1), 0, NBIN - 1).astype(jnp.int32),
        "masses": jnp.clip(jax.random.uniform(arg_keys[4], (N_DP, GE), jnp.float32, -1.5, 1.5) * shard_levels(arg_keys[4], (N_DP, GE), ((0, 4),), -0.4, 0.0), -1.5, 1.5),
        "gain_attn": jnp.clip(1.0 + 0.15 * jax.random.normal(arg_keys[5], (LAYERS, D), jnp.float32), 0.25, 1.75),
        "w_qkv": gaussian(arg_keys[6], (LAYERS, D, 3 * D), D ** -0.5, 0.375),
        "w_out": gaussian(arg_keys[7], (LAYERS, D, D), D ** -0.5, 0.375),
        "pair_table": gaussian(arg_keys[8], (LAYERS, NBIN, H), 1.0, 4.0, (), jnp.float32),
        "gain_ffn": jnp.clip(1.0 + 0.15 * jax.random.normal(arg_keys[9], (LAYERS, D), jnp.float32), 0.25, 1.75),
        "w_up": gaussian(arg_keys[10], (LAYERS, D, FF), D ** -0.5, 0.375),
        "w_down": gaussian(arg_keys[11], (LAYERS, FF, D), FF ** -0.5, 0.1875),
        "w_phi": gaussian(arg_keys[12], (D, DP), D ** -0.5, 0.375),
        "w_mean": gaussian(arg_keys[13], (DP,), DP ** -0.5, 0.375, (), jnp.float32),
        "w_scale": gaussian(arg_keys[14], (DP,), DP ** -0.5, 0.375, (), jnp.float32),
    }


def normalize(stream, gain_vec):
    average = lax.optimization_barrier(jnp.mean(stream, axis=-1, keepdims=True))
    centred = stream - average
    variance = lax.optimization_barrier(jnp.mean(centred * centred, axis=-1, keepdims=True))
    return centred * lax.rsqrt(variance + 1e-05) * gain_vec

def encoder(packed, jets, lengths, pair_bins):
    gain_attn, w_qkv, w_out, pair_table, gain_ffn, w_up, w_down, w_phi = packed
    count_jets, slots, width = jets.shape
    heads = pair_table.shape[2]
    head_dim = width // heads
    live_keys = jnp.arange(slots, dtype=jnp.int32)[None, :] < lengths[:, None]
    bin_onehot = (pair_bins[..., None] == jnp.arange(pair_table.shape[1], dtype=jnp.int32)).astype(jnp.float32)
    stream = jets
    for depth in range(w_qkv.shape[0]):
        pair_bias = jnp.einsum('jqkb,bh->jhqk', bin_onehot, pair_table[depth], precision=lax.Precision.HIGHEST)
        normed = normalize(stream.astype(jnp.float32), gain_attn[depth]).astype(jnp.bfloat16).reshape(count_jets * slots, width)
        projected = jnp.dot(normed, w_qkv[depth], preferred_element_type=jnp.float32).astype(jnp.bfloat16)
        projected = projected.reshape(count_jets, slots, 3, heads, head_dim)
        queries = projected[:, :, 0].astype(jnp.float32)
        key_rows = projected[:, :, 1].astype(jnp.float32)
        value_rows = projected[:, :, 2].astype(jnp.float32)
        scores = jnp.einsum('jqhe,jkhe->jhqk', queries, key_rows) / math.sqrt(head_dim) + pair_bias
        scores = jnp.where(live_keys[:, None, None, :], scores, -1e+30)
        attend = jax.nn.softmax(scores, axis=-1).astype(jnp.bfloat16)
        context = jnp.einsum('jhqk,jkhe->jqhe', attend.astype(jnp.float32), value_rows).astype(jnp.bfloat16)
        context = context.reshape(count_jets * slots, width)
        middle = stream.astype(jnp.float32).reshape(count_jets * slots, width) + jnp.dot(context, w_out[depth], preferred_element_type=jnp.float32)
        normed = normalize(middle, gain_ffn[depth]).astype(jnp.bfloat16)
        hidden = jax.nn.gelu(jnp.dot(normed, w_up[depth], preferred_element_type=jnp.float32)).astype(jnp.bfloat16)
        stream = (middle + jnp.dot(hidden, w_down[depth], preferred_element_type=jnp.float32)).astype(jnp.bfloat16)
        stream = stream.reshape(count_jets, slots, width)
    pooled = lax.optimization_barrier(jnp.sum(jnp.where(live_keys[..., None], stream.astype(jnp.float32), 0.0), axis=1))
    pooled = (pooled / lengths[:, None].astype(jnp.float32)).astype(jnp.bfloat16)
    return jax.nn.gelu(jnp.dot(pooled, w_phi, preferred_element_type=jnp.float32))

def flow_head(head_weights, summed, number, masses):
    w_mean, w_scale = head_weights
    average = summed / number[..., None]
    centre = lax.optimization_barrier(jnp.sum(average * w_mean, axis=-1))
    log_width = lax.optimization_barrier(jnp.sum(average * w_scale, axis=-1))
    return 0.5 * jnp.square((masses - centre) * jnp.exp(-log_width)) + log_width

def reference(embed, counts, member, bins, masses, gain_attn, w_qkv, w_out, pair_table, gain_ffn, w_up, w_down, w_phi, w_mean, w_scale):
    packed = (gain_attn, w_qkv, w_out, pair_table, gain_ffn, w_up, w_down, w_phi)
    blocks = N_DP * N_ENS
    emb_blocks = embed.reshape(blocks, JET_DEV, NC, D)
    count_blocks = counts.reshape(blocks, JET_DEV)
    bin_blocks = bins.reshape(blocks, JET_DEV, NC, NC)

    def forward_block(items):
        return encoder(packed, items[0], items[1], items[2])
    phi_all = lax.map(forward_block, (emb_blocks, count_blocks, bin_blocks))
    phi_all = phi_all.reshape(N_DP, N_ENS, JET_DEV, DP)
    group_onehot = (member.reshape(N_DP, N_ENS, JET_DEV)[..., None] == jnp.arange(GE, dtype=jnp.int32)).astype(jnp.float32)
    summed = jnp.einsum('gnje,gnjp->gep', group_onehot, phi_all, precision=lax.Precision.HIGHEST)
    number = lax.optimization_barrier(jnp.sum(group_onehot, axis=(1, 2)))

    def head_part(head_weights, summed_in):
        return flow_head(head_weights, summed_in, number, masses)
    neg_loglik, back_head = jax.vjp(head_part, (w_mean, w_scale), summed)
    head_grads, summed_grad = back_head(jnp.full(neg_loglik.shape, 1.0 / (N_DP * GE), jnp.float32))
    phi_grad = jnp.einsum('gnje,gep->gnjp', group_onehot, summed_grad, precision=lax.Precision.HIGHEST)
    phi_grad = phi_grad.reshape(blocks, JET_DEV, DP)

    def backward_block(carry, items):

        def local_part(params_in):
            return encoder(params_in, items[0], items[1], items[2])
        unused, back_trunk = jax.vjp(local_part, packed)
        partial_grads = back_trunk(items[3])[0]
        return (jax.tree.map(lambda total, piece: total + piece.astype(jnp.float32), carry, partial_grads), None)
    start = jax.tree.map(lambda weight_arr: jnp.zeros(weight_arr.shape, jnp.float32), packed)
    grads, unused = lax.scan(backward_block, start, (emb_blocks, count_blocks, bin_blocks, phi_grad))
    return (neg_loglik, grads[0], grads[1], grads[2], grads[3], grads[4], grads[5], grads[6], grads[7], head_grads[0], head_grads[1])
```

```python
import functools
import math

import jax
import jax.numpy as jnp
from jax import lax
from jax.experimental import pallas as pl
from jax.experimental.pallas import tpu as pltpu
from jax.sharding import PartitionSpec as P

F32 = jnp.float32
BF16 = jnp.bfloat16
TOGETHER = 2
GELU_A = math.sqrt(2.0 / math.pi)
GELU_B = 0.044715


def dot(a, b, ca=1, cb=0):
    return lax.dot_general(a, b, (((ca,), (cb,)), ((), ())), preferred_element_type=F32)


def center(rows):
    average = jnp.mean(rows, axis=-1, keepdims=True)
    centred = rows - average
    variance = jnp.mean(centred * centred, axis=-1, keepdims=True)
    inverse = lax.rsqrt(variance + 1e-05)
    return centred * inverse, inverse


def center_back(d_hat, hat, inverse):
    first = jnp.mean(d_hat, axis=-1, keepdims=True)
    second = jnp.mean(d_hat * hat, axis=-1, keepdims=True)
    return inverse * (d_hat - first - hat * second)


def gelu_tanh(u):
    return jnp.tanh(GELU_A * (u + GELU_B * (u * u * u)))


def head_lanes(slots, width, heads):
    head_of = lax.broadcasted_iota(jnp.int32, (slots, width), 1) // (width // heads)
    return [head_of == h for h in range(heads)]


def spread(rows, lanes):
    return jnp.concatenate([rows * m.astype(F32).astype(BF16) for m in lanes], axis=0)


def collect(stacked, lanes, slots):
    out = stacked[0:slots]
    for h in range(1, len(lanes)):
        out = jnp.where(lanes[h], stacked[h * slots : (h + 1) * slots], out)
    return out


def forward_kernel(
    counts, table, x_ref, bins_ref, g1, w_qkv, w_out, g2, w_up, w_down,
    proj_o, att_o, ctx_o, mid_o, pooled_o,
):
    step = pl.program_id(0)
    slots = bins_ref.shape[1]
    width = x_ref.shape[1]
    heads = table.shape[1]
    scale = 1.0 / math.sqrt(width // heads)
    lanes = head_lanes(slots, width, heads)
    x = x_ref[...].astype(F32)
    hat, _ = center(x)
    normed = (hat * g1[...]).astype(BF16)
    proj = dot(normed, w_qkv[...]).astype(BF16)
    proj_o[...] = proj
    for j in range(TOGETHER):
        length = counts[step * TOGETHER + j]
        rows = slice(j * slots, (j + 1) * slots)
        queries = spread(proj[rows, 0:width], lanes)
        keys = proj[rows, width : 2 * width]
        values = proj[rows, 2 * width : 3 * width]
        raw = dot(keys, queries, 1, 1)
        levels = bins_ref[j].T
        bit0 = (levels & 1) == 1
        bit1 = (levels & 2) == 2
        bit2 = (levels & 4) == 4
        live = lax.broadcasted_iota(jnp.int32, (slots, slots), 0) < length
        pieces = []
        for h in range(heads):
            pair = [jnp.where(bit0, table[2 * i + 1, h], table[2 * i, h]) for i in range(4)]
            low = jnp.where(bit1, pair[1], pair[0])
            high = jnp.where(bit1, pair[3], pair[2])
            bias = jnp.where(bit2, high, low)
            score = raw[:, h * slots : (h + 1) * slots] * scale + bias
            score = jnp.where(live, score, -1e30)
            top = jnp.max(score, axis=0, keepdims=True)
            power = jnp.exp(score - top)
            total = jnp.sum(power, axis=0, keepdims=True)
            pieces.append((power * (1.0 / total)).astype(BF16))
        attend = jnp.concatenate(pieces, axis=1)
        att_o[j] = attend
        context = collect(dot(attend, values, 0, 0), lanes, slots)
        ctx_o[rows, :] = context.astype(BF16)
    middle = x + dot(ctx_o[...], w_out[...])
    mid_o[...] = middle
    hat, _ = center(middle)
    normed = (hat * g2[...]).astype(BF16)
    u = dot(normed, w_up[...])
    hidden = (0.5 * u * (1.0 + gelu_tanh(u))).astype(BF16)
    stream = (middle + dot(hidden, w_down[...])).astype(BF16).astype(F32)
    for j in range(TOGETHER):
        length = counts[step * TOGETHER + j]
        live = lax.broadcasted_iota(jnp.int32, (slots, width), 0) < length
        kept = jnp.where(live, stream[j * slots : (j + 1) * slots], 0.0)
        pooled_o[0, j : j + 1, :] = jnp.sum(kept, axis=0, keepdims=True)


def backward_kernel(
    counts, x_ref, bins_ref, proj_ref, att_ref, ctx_ref, mid_ref, back_ref, tail_ref,
    g1, w_qkv, w_out, g2, w_up, w_down,
    flat_o, table_acc,
):
    step = pl.program_id(0)
    slots = bins_ref.shape[1]
    width = x_ref.shape[1]
    ffn = w_up.shape[1]
    heads = att_ref.shape[2] // slots
    levels_n = table_acc.shape[0] // (8 * heads)
    scale = 1.0 / math.sqrt(width // heads)
    lanes = head_lanes(slots, width, heads)
    base_out = 3 * width
    base_up = base_out + width
    base_down = base_up + ffn
    base_phi = base_down + ffn
    base_tail = base_phi + width

    @pl.when(step == 0)
    def _():
        flat_o[...] = jnp.zeros(flat_o.shape, F32)
        table_acc[...] = jnp.zeros(table_acc.shape, F32)

    parts = []
    for j in range(TOGETHER):
        length = counts[step * TOGETHER + j]
        live = lax.broadcasted_iota(jnp.int32, (slots, width), 0) < length
        parts.append(jnp.where(live, back_ref[0, j : j + 1, :], 0.0))
    d_stream = jnp.concatenate(parts, axis=0)
    d_stream_b = d_stream.astype(BF16)
    middle = mid_ref[...]
    hat2, inverse2 = center(middle)
    normed2 = (hat2 * g2[...]).astype(BF16)
    d_normed = jnp.zeros(middle.shape, F32)
    for c in range(0, ffn, width):
        cols = slice(c, c + width)
        u = dot(normed2, w_up[:, cols])
        t = gelu_tanh(u)
        hidden = (0.5 * u * (1.0 + t)).astype(BF16)
        d_hidden = dot(d_stream_b, w_down[cols, :], 1, 1).astype(BF16).astype(F32)
        slope = 0.5 * (1.0 + t) + 0.5 * u * (1.0 - t * t) * (
            GELU_A * (1.0 + 3.0 * GELU_B * (u * u))
        )
        d_u = (d_hidden * slope).astype(BF16)
        flat_o[base_down + c : base_down + c + width, :] += dot(hidden, d_stream_b, 0, 0)
        flat_o[base_up + c : base_up + c + width, :] += dot(normed2, d_u, 0, 0)
        d_normed = d_normed + dot(d_u, w_up[:, cols], 1, 1)
    d_normed = d_normed.astype(BF16).astype(F32)
    flat_o[base_tail + 1 : base_tail + 2, :] += jnp.sum(d_normed * hat2, axis=0, keepdims=True)
    d_middle = d_stream_b.astype(F32) + center_back(d_normed * g2[...], hat2, inverse2)
    d_middle_b = d_middle.astype(BF16)
    d_context = dot(d_middle_b, w_out[...], 1, 1).astype(BF16)
    flat_o[base_out : base_out + width, :] += dot(ctx_ref[...], d_middle_b, 0, 0)

    d_rows = []
    for j in range(TOGETHER):
        rows = slice(j * slots, (j + 1) * slots)
        queries = spread(proj_ref[rows, 0:width], lanes)
        keys = proj_ref[rows, width : 2 * width]
        values = proj_ref[rows, 2 * width : 3 * width]
        d_ctx = spread(d_context[rows], lanes)
        attend = att_ref[j]
        d_att = dot(values, d_ctx, 1, 1)
        d_values = dot(attend, d_ctx)
        levels = bins_ref[j].T
        pieces = []
        for h in range(heads):
            cols = slice(h * slots, (h + 1) * slots)
            a = attend[:, cols].astype(F32)
            d_a = d_att[:, cols]
            inner = jnp.sum(a * d_a, axis=0, keepdims=True)
            d_s = a * (d_a - inner)
            for b in range(levels_n):
                held = jnp.where(levels == b, d_s, 0.0)
                at = (b * heads + h) * 8
                table_acc[at : at + 8, :] += jnp.sum(held.reshape(slots // 8, 8, slots), axis=0)
            pieces.append((d_s * scale).astype(BF16))
        d_score = jnp.concatenate(pieces, axis=1)
        d_keys = dot(d_score, queries)
        d_queries = collect(dot(d_score, keys, 0, 0), lanes, slots)
        d_rows.append(
            jnp.concatenate(
                [d_queries.astype(BF16), d_keys.astype(BF16), d_values.astype(BF16)], axis=1
            )
        )
    d_proj = jnp.concatenate(d_rows, axis=0)
    hat1, _ = center(x_ref[...].astype(F32))
    normed1 = (hat1 * g1[...]).astype(BF16)
    for c in range(3):
        cols = slice(c * width, (c + 1) * width)
        flat_o[c * width : (c + 1) * width, :] += dot(normed1, d_proj[:, cols], 0, 0)
    d_first = dot(d_proj, w_qkv[...], 1, 1).astype(BF16).astype(F32)
    flat_o[base_tail : base_tail + 1, :] += jnp.sum(d_first * hat1, axis=0, keepdims=True)

    @pl.when(step == pl.num_programs(0) - 1)
    def _():
        flat_o[0:base_phi, :] = flat_o[0:base_phi, :].astype(BF16).astype(F32)
        flat_o[base_phi:base_tail, :] = tail_ref[0:width, :]
        flat_o[base_tail + 2 : base_tail + 4, :] = tail_ref[width : width + 2, :]
        count = levels_n * heads
        flat_o[base_tail + 8 : base_tail + 8 + count, 0:slots] = jnp.sum(
            table_acc[...].reshape(count, 8, slots), axis=1
        )


def whole_block(shape):
    return pl.BlockSpec(shape, lambda i: (0,) * len(shape))


def row_block(shape):
    return pl.BlockSpec(shape, lambda i: (i,) + (0,) * (len(shape) - 1))


def flow_head(head_weights, summed, number, masses):
    w_mean, w_scale = head_weights
    average = summed / number[..., None]
    centre = jnp.sum(average * w_mean, axis=-1)
    log_width = jnp.sum(average * w_scale, axis=-1)
    return 0.5 * jnp.square((masses - centre) * jnp.exp(-log_width)) + log_width


def total_over_all(flat):
    return lax.psum(flat, ("dp", "ens"))


def shards(
    embed, counts, member, bins, masses,
    gain_attn, w_qkv, w_out, pair_table, gain_ffn, w_up, w_down, w_phi, w_mean, w_scale,
):
    jets_n, slots, width = embed.shape[1:]
    heads = pair_table.shape[2]
    levels_n = pair_table.shape[1]
    ffn = w_up.shape[2]
    lengths = counts[0]
    pair_bins = bins[0]
    group_masses = masses[0]
    groups_total = group_masses.shape[0]
    steps = jets_n // TOGETHER
    block = TOGETHER * slots
    x = embed[0].reshape(jets_n * slots, width)
    weights = (gain_attn, w_qkv[0], w_out[0], gain_ffn, w_up[0], w_down[0])
    weight_specs = [whole_block(w.shape) for w in weights]
    smem = pl.BlockSpec(memory_space=pltpu.SMEM)
    params = pltpu.CompilerParams(
        dimension_semantics=("arbitrary",), vmem_limit_bytes=50 * 1024 * 1024
    )
    bins_spec = row_block((TOGETHER, slots, slots))
    kept_specs = [
        row_block((block, 3 * width)),
        row_block((TOGETHER, slots, heads * slots)),
        row_block((block, width)),
        row_block((block, width)),
    ]
    proj, att, ctx, mid, pooled_sum = pl.pallas_call(
        forward_kernel,
        grid=(steps,),
        in_specs=[smem, smem, row_block((block, width)), bins_spec] + weight_specs,
        out_specs=kept_specs + [row_block((1, TOGETHER, width))],
        out_shape=[
            jax.ShapeDtypeStruct((jets_n * slots, 3 * width), BF16),
            jax.ShapeDtypeStruct((jets_n, slots, heads * slots), BF16),
            jax.ShapeDtypeStruct((jets_n * slots, width), BF16),
            jax.ShapeDtypeStruct((jets_n * slots, width), F32),
            jax.ShapeDtypeStruct((steps, TOGETHER, width), F32),
        ],
        compiler_params=params,
        name="forward",
    )(lengths, pair_table[0], x, pair_bins, *weights)

    inverse_length = lengths[:, None].astype(F32)
    pooled = (pooled_sum.reshape(jets_n, width) / inverse_length).astype(BF16)

    def phi_part(pooled_in, w_in):
        return jax.nn.gelu(jnp.dot(pooled_in, w_in, preferred_element_type=F32))

    phi, back_phi = jax.vjp(phi_part, pooled, w_phi)
    group_onehot = (member[0][:, None] == jnp.arange(groups_total, dtype=jnp.int32)).astype(F32)
    partial_sum = jnp.dot(group_onehot.T, phi, precision=lax.Precision.HIGHEST)
    tally = jnp.sum(group_onehot, axis=0)
    joined = jnp.concatenate(
        [partial_sum, jnp.broadcast_to(tally[:, None], (groups_total, 128))], axis=1
    )
    joined = lax.psum(joined, "ens")
    summed, number = joined[:, :width], joined[:, width]

    def head_part(head_weights, summed_in):
        return flow_head(head_weights, summed_in, number, group_masses)

    neg_loglik, back_head = jax.vjp(head_part, (w_mean, w_scale), summed)
    scale_total = 1.0 / (lax.axis_size("dp") * groups_total)
    head_grads, summed_grad = back_head(jnp.full(neg_loglik.shape, scale_total, F32))
    phi_grad = jnp.dot(group_onehot, summed_grad, precision=lax.Precision.HIGHEST)
    d_pooled, d_phi = back_phi(phi_grad)
    d_pooled = (d_pooled.astype(F32) / inverse_length).reshape(steps, TOGETHER, width)
    share = 1.0 / lax.axis_size("ens")
    tail = jnp.concatenate(
        [
            d_phi.astype(F32),
            head_grads[0][None] * share,
            head_grads[1][None] * share,
            jnp.zeros((6, width), F32),
        ],
        axis=0,
    )

    base_tail = 3 * width + width + 2 * ffn + width
    unit = 8 * lax.axis_size("dp") * lax.axis_size("ens")
    used = base_tail + 8 + levels_n * heads
    flat_rows = (used + unit - 1) // unit * unit
    flat = pl.pallas_call(
        backward_kernel,
        grid=(steps,),
        in_specs=[smem, row_block((block, width)), bins_spec]
        + kept_specs
        + [row_block((1, TOGETHER, width)), whole_block(tail.shape)]
        + weight_specs,
        out_specs=whole_block((flat_rows, width)),
        out_shape=jax.ShapeDtypeStruct((flat_rows, width), F32),
        scratch_shapes=[pltpu.VMEM((levels_n * heads * 8, slots), F32)],
        compiler_params=params,
        name="backward",
    )(lengths, x, pair_bins, proj, att, ctx, mid, d_pooled, tail, *weights)

    total = total_over_all(flat)
    g_qkv = jnp.concatenate([total[i * width : (i + 1) * width] for i in range(3)], axis=1)
    at = 3 * width
    g_out = total[at : at + width]
    at += width
    g_up = jnp.concatenate(
        [total[at + i : at + i + width] for i in range(0, ffn, width)], axis=1
    )
    at += ffn
    g_down = total[at : at + ffn]
    at += ffn
    g_phi = total[at : at + width]
    small = total[base_tail : base_tail + 8 + levels_n * heads]
    g_table = jnp.sum(small[8:, :slots], axis=1).reshape(1, levels_n, heads)
    return (
        neg_loglik[None, :],
        small[0:1],
        g_qkv[None],
        g_out[None],
        g_table,
        small[1:2],
        g_up[None],
        g_down[None],
        g_phi,
        small[2],
        small[3],
    )


def solution(mesh):
    in_specs = (
        P("dp", "ens", None, None),
        P("dp", "ens"),
        P("dp", "ens"),
        P("dp", "ens", None, None),
        P("dp", None),
    ) + (P(),) * 10
    out_specs = (P("dp", None),) + (P(),) * 10
    return jax.shard_map(shards, mesh=mesh, in_specs=in_specs, out_specs=out_specs, check_vma=False)
```

```python
import functools
import math

import jax
import jax.numpy as jnp
from jax import lax
from jax.experimental import pallas as pl
from jax.experimental.pallas import tpu as pltpu
from jax.sharding import PartitionSpec as P

F32 = jnp.float32
BF16 = jnp.bfloat16
TOGETHER = 2
GELU_A = math.sqrt(2.0 / math.pi)
GELU_B = 0.044715


def dot(a, b, ca=1, cb=0):
    return lax.dot_general(a, b, (((ca,), (cb,)), ((), ())), preferred_element_type=F32)


def center(rows):
    average = jnp.mean(rows, axis=-1, keepdims=True)
    centred = rows - average
    variance = jnp.mean(centred * centred, axis=-1, keepdims=True)
    inverse = lax.rsqrt(variance + 1e-05)
    return centred * inverse, inverse


def center_back(d_hat, hat, inverse):
    first = jnp.mean(d_hat, axis=-1, keepdims=True)
    second = jnp.mean(d_hat * hat, axis=-1, keepdims=True)
    return inverse * (d_hat - first - hat * second)


def gelu_tanh(u):
    return jnp.tanh(GELU_A * (u + GELU_B * (u * u * u)))


def head_lanes(slots, width, heads):
    head_of = lax.broadcasted_iota(jnp.int32, (slots, width), 1) // (width // heads)
    return [head_of == h for h in range(heads)]


def spread(rows, lanes):
    return jnp.concatenate([rows * m.astype(F32).astype(BF16) for m in lanes], axis=0)


def collect(stacked, lanes, slots):
    out = stacked[0:slots]
    for h in range(1, len(lanes)):
        out = jnp.where(lanes[h], stacked[h * slots : (h + 1) * slots], out)
    return out


def forward_kernel(
    counts, table, x_ref, bins_ref, g1, w_qkv, w_out, g2, w_up, w_down,
    proj_o, att_o, ctx_o, mid_o, pooled_o,
):
    step = pl.program_id(0)
    slots = bins_ref.shape[1]
    width = x_ref.shape[1]
    heads = table.shape[1]
    scale = 1.0 / math.sqrt(width // heads)
    lanes = head_lanes(slots, width, heads)
    x = x_ref[...].astype(F32)
    hat, _ = center(x)
    normed = (hat * g1[...]).astype(BF16)
    proj = dot(normed, w_qkv[...]).astype(BF16)
    proj_o[...] = proj
    for j in range(TOGETHER):
        length = counts[step * TOGETHER + j]
        rows = slice(j * slots, (j + 1) * slots)
        queries = spread(proj[rows, 0:width], lanes)
        keys = proj[rows, width : 2 * width]
        values = proj[rows, 2 * width : 3 * width]
        raw = dot(keys, queries, 1, 1)
        levels = bins_ref[j].T
        bit0 = (levels & 1) == 1
        bit1 = (levels & 2) == 2
        bit2 = (levels & 4) == 4
        live = lax.broadcasted_iota(jnp.int32, (slots, slots), 0) < length
        pieces = []
        for h in range(heads):
            pair = [jnp.where(bit0, table[2 * i + 1, h], table[2 * i, h]) for i in range(4)]
            low = jnp.where(bit1, pair[1], pair[0])
            high = jnp.where(bit1, pair[3], pair[2])
            bias = jnp.where(bit2, high, low)
            score = raw[:, h * slots : (h + 1) * slots] * scale + bias
            score = jnp.where(live, score, -1e30)
            top = jnp.max(score, axis=0, keepdims=True)
            power = jnp.exp(score - top)
            total = jnp.sum(power, axis=0, keepdims=True)
            pieces.append((power * (1.0 / total)).astype(BF16))
        attend = jnp.concatenate(pieces, axis=1)
        att_o[j] = attend
        context = collect(dot(attend, values, 0, 0), lanes, slots)
        ctx_o[rows, :] = context.astype(BF16)
    middle = x + dot(ctx_o[...], w_out[...])
    mid_o[...] = middle
    hat, _ = center(middle)
    normed = (hat * g2[...]).astype(BF16)
    u = dot(normed, w_up[...])
    hidden = (0.5 * u * (1.0 + gelu_tanh(u))).astype(BF16)
    stream = (middle + dot(hidden, w_down[...])).astype(BF16).astype(F32)
    for j in range(TOGETHER):
        length = counts[step * TOGETHER + j]
        live = lax.broadcasted_iota(jnp.int32, (slots, width), 0) < length
        kept = jnp.where(live, stream[j * slots : (j + 1) * slots], 0.0)
        pooled_o[0, j : j + 1, :] = jnp.sum(kept, axis=0, keepdims=True)


def backward_kernel(
    counts, x_ref, bins_ref, proj_ref, att_ref, ctx_ref, mid_ref, back_ref, tail_ref,
    g1, w_qkv, w_out, g2, w_up, w_down,
    flat_o, table_acc,
):
    step = pl.program_id(0)
    slots = bins_ref.shape[1]
    width = x_ref.shape[1]
    ffn = w_up.shape[1]
    heads = att_ref.shape[2] // slots
    levels_n = table_acc.shape[0] // (8 * heads)
    scale = 1.0 / math.sqrt(width // heads)
    lanes = head_lanes(slots, width, heads)
    base_out = 3 * width
    base_up = base_out + width
    base_down = base_up + ffn
    base_phi = base_down + ffn
    base_tail = base_phi + width

    @pl.when(step == 0)
    def _():
        flat_o[...] = jnp.zeros(flat_o.shape, F32)
        table_acc[...] = jnp.zeros(table_acc.shape, F32)

    parts = []
    for j in range(TOGETHER):
        length = counts[step * TOGETHER + j]
        live = lax.broadcasted_iota(jnp.int32, (slots, width), 0) < length
        parts.append(jnp.where(live, back_ref[0, j : j + 1, :], 0.0))
    d_stream = jnp.concatenate(parts, axis=0)
    d_stream_b = d_stream.astype(BF16)
    middle = mid_ref[...]
    hat2, inverse2 = center(middle)
    normed2 = (hat2 * g2[...]).astype(BF16)
    d_normed = jnp.zeros(middle.shape, F32)
    for c in range(0, ffn, width):
        cols = slice(c, c + width)
        u = dot(normed2, w_up[:, cols])
        t = gelu_tanh(u)
        hidden = (0.5 * u * (1.0 + t)).astype(BF16)
        d_hidden = dot(d_stream_b, w_down[cols, :], 1, 1).astype(BF16).astype(F32)
        slope = 0.5 * (1.0 + t) + 0.5 * u * (1.0 - t * t) * (
            GELU_A * (1.0 + 3.0 * GELU_B * (u * u))
        )
        d_u = (d_hidden * slope).astype(BF16)
        flat_o[base_down + c : base_down + c + width, :] += dot(hidden, d_stream_b, 0, 0)
        flat_o[base_up + c : base_up + c + width, :] += dot(normed2, d_u, 0, 0)
        d_normed = d_normed + dot(d_u, w_up[:, cols], 1, 1)
    d_normed = d_normed.astype(BF16).astype(F32)
    flat_o[base_tail + 1 : base_tail + 2, :] += jnp.sum(d_normed * hat2, axis=0, keepdims=True)
    d_middle = d_stream_b.astype(F32) + center_back(d_normed * g2[...], hat2, inverse2)
    d_middle_b = d_middle.astype(BF16)
    d_context = dot(d_middle_b, w_out[...], 1, 1).astype(BF16)
    flat_o[base_out : base_out + width, :] += dot(ctx_ref[...], d_middle_b, 0, 0)

    d_rows = []
    for j in range(TOGETHER):
        rows = slice(j * slots, (j + 1) * slots)
        queries = spread(proj_ref[rows, 0:width], lanes)
        keys = proj_ref[rows, width : 2 * width]
        values = proj_ref[rows, 2 * width : 3 * width]
        d_ctx = spread(d_context[rows], lanes)
        attend = att_ref[j]
        d_att = dot(values, d_ctx, 1, 1)
        d_values = dot(attend, d_ctx)
        levels = bins_ref[j].T
        pieces = []
        for h in range(heads):
            cols = slice(h * slots, (h + 1) * slots)
            a = attend[:, cols].astype(F32)
            d_a = d_att[:, cols]
            inner = jnp.sum(a * d_a, axis=0, keepdims=True)
            d_s = a * (d_a - inner)
            for b in range(levels_n):
                held = jnp.where(levels == b, d_s, 0.0)
                at = (b * heads + h) * 8
                table_acc[at : at + 8, :] += jnp.sum(held.reshape(slots // 8, 8, slots), axis=0)
            pieces.append((d_s * scale).astype(BF16))
        d_score = jnp.concatenate(pieces, axis=1)
        d_keys = dot(d_score, queries)
        d_queries = collect(dot(d_score, keys, 0, 0), lanes, slots)
        d_rows.append(
            jnp.concatenate(
                [d_queries.astype(BF16), d_keys.astype(BF16), d_values.astype(BF16)], axis=1
            )
        )
    d_proj = jnp.concatenate(d_rows, axis=0)
    hat1, _ = center(x_ref[...].astype(F32))
    normed1 = (hat1 * g1[...]).astype(BF16)
    for c in range(3):
        cols = slice(c * width, (c + 1) * width)
        flat_o[c * width : (c + 1) * width, :] += dot(normed1, d_proj[:, cols], 0, 0)
    d_first = dot(d_proj, w_qkv[...], 1, 1).astype(BF16).astype(F32)
    flat_o[base_tail : base_tail + 1, :] += jnp.sum(d_first * hat1, axis=0, keepdims=True)

    @pl.when(step == pl.num_programs(0) - 1)
    def _():
        flat_o[0:base_phi, :] = flat_o[0:base_phi, :].astype(BF16).astype(F32)
        flat_o[base_phi:base_tail, :] = tail_ref[0:width, :]
        flat_o[base_tail + 2 : base_tail + 4, :] = tail_ref[width : width + 2, :]
        count = levels_n * heads
        flat_o[base_tail + 8 : base_tail + 8 + count, 0:slots] = jnp.sum(
            table_acc[...].reshape(count, 8, slots), axis=1
        )


def whole_block(shape):
    return pl.BlockSpec(shape, lambda i: (0,) * len(shape))


def row_block(shape):
    return pl.BlockSpec(shape, lambda i: (i,) + (0,) * (len(shape) - 1))


def flow_head(head_weights, summed, number, masses):
    w_mean, w_scale = head_weights
    average = summed / number[..., None]
    centre = jnp.sum(average * w_mean, axis=-1)
    log_width = jnp.sum(average * w_scale, axis=-1)
    return 0.5 * jnp.square((masses - centre) * jnp.exp(-log_width)) + log_width


MESH = pl.DeviceIdType.MESH


def greet(partners):
    barrier = pltpu.get_barrier_semaphore()
    for partner in partners:
        pl.semaphore_signal(barrier, inc=1, device_id=partner, device_id_type=MESH)
    pl.semaphore_wait(barrier, len(partners))


def reduce_kernel(ens, x_ref, out_ref, work, full, in_a, in_b, in_c, in_d, send, recv, own):
    d, e = lax.axis_index("dp"), lax.axis_index("ens")
    core, xb = d % 2, d // 2
    yb, z = e % 2, e // 2
    line = ens // 2
    rows = x_ref.shape[0]
    size_a, size_b, size_c = rows // 2, rows // 4, rows // 8
    size_d = size_c // line

    def span(start, size):
        return pl.ds(pl.multiple_of(start, 8), size)

    bit_b = (1 - core) * xb + core * yb
    bit_c = (1 - core) * yb + core * xb
    step_x = 2 * (1 - 2 * xb)
    step_y = 1 - 2 * yb
    mate_a = (d + 1 - 2 * core, e)
    mate_b = (d + (1 - core) * step_x, e + core * step_y)
    mate_c = (d + core * step_x, e + (1 - core) * step_y)
    mates_d = [(d, (z + k) % line * 2 + yb) for k in range(1, line)]
    greet([mate_a, mate_b, mate_c] + mates_d)

    def copy(source, target, number, mate):
        return pltpu.make_async_remote_copy(
            src_ref=source, dst_ref=target, send_sem=send.at[number], recv_sem=recv.at[number],
            device_id=mate, device_id_type=MESH,
        )

    start_a = core * size_a
    start_b = start_a + bit_b * size_b
    start_c = start_b + bit_c * size_c
    start_d = start_c + z * size_d

    there = copy(x_ref.at[span((1 - core) * size_a, size_a)], in_a, 0, mate_a)
    there.start()
    there.wait()
    part = span(start_a, size_a)
    work[part, :] = x_ref[part, :] + in_a[...]

    there = copy(work.at[span(start_a + (1 - bit_b) * size_b, size_b)], in_b, 1, mate_b)
    there.start()
    there.wait()
    part = span(start_b, size_b)
    work[part, :] = work[part, :] + in_b[...]

    there = copy(work.at[span(start_b + (1 - bit_c) * size_c, size_c)], in_c, 2, mate_c)
    there.start()
    there.wait()
    part = span(start_c, size_c)
    work[part, :] = work[part, :] + in_c[...]

    group = []
    for k in range(1, line):
        piece = span(start_c + (z + k) % line * size_d, size_d)
        group.append(copy(work.at[piece], in_d.at[k - 1], 2 + k, mates_d[k - 1]))
    for there in group:
        there.start()
    for there in group:
        there.wait()
    part = span(start_d, size_d)
    total = work[part, :]
    for k in range(1, line):
        total = total + in_d[k - 1]
    full[part, :] = total

    group = [
        copy(full.at[part], full.at[part], 1 + line + k, mates_d[k - 1]) for k in range(1, line)
    ]
    for there in group:
        there.start()
    for there in group:
        there.wait()
    last = 2 * line + 1
    for number, start, size, mate in (
        (last, start_c, size_c, mate_c),
        (last + 1, start_b, size_b, mate_b),
        (last + 2, start_a, size_a, mate_a),
    ):
        part = span(start, size)
        there = copy(full.at[part], full.at[part], number, mate)
        there.start()
        there.wait()
    back = pltpu.make_async_copy(full, out_ref, own)
    back.start()
    back.wait()


def total_over_all(flat):
    ens = lax.axis_size("ens")
    rows, width = flat.shape
    line = ens // 2
    count = 2 * line + 4
    return pl.pallas_call(
        functools.partial(reduce_kernel, ens),
        out_shape=jax.ShapeDtypeStruct(flat.shape, F32),
        in_specs=[pl.BlockSpec(memory_space=pltpu.VMEM)],
        out_specs=pl.BlockSpec(memory_space=pl.ANY),
        scratch_shapes=[
            pltpu.VMEM((rows, width), F32),
            pltpu.VMEM((rows, width), F32),
            pltpu.VMEM((rows // 2, width), F32),
            pltpu.VMEM((rows // 4, width), F32),
            pltpu.VMEM((rows // 8, width), F32),
            pltpu.VMEM((line - 1, rows // 8 // line, width), F32),
            pltpu.SemaphoreType.DMA((count,)),
            pltpu.SemaphoreType.DMA((count,)),
            pltpu.SemaphoreType.DMA,
        ],
        compiler_params=pltpu.CompilerParams(
            collective_id=0, has_side_effects=True, vmem_limit_bytes=40 * 1024 * 1024
        ),
        name="reduce",
    )(flat)


def small_kernel(ens, x_ref, out_ref, slots, send, recv):
    d, e = lax.axis_index("dp"), lax.axis_index("ens")
    mates = [(d, (e + k) % ens) for k in range(1, ens)]
    greet(mates)
    copies = []
    for k in range(1, ens):
        copies.append(
            pltpu.make_async_remote_copy(
                src_ref=x_ref, dst_ref=slots.at[e], send_sem=send.at[k], recv_sem=recv.at[k],
                device_id=mates[k - 1], device_id_type=MESH,
            )
        )
    for there in copies:
        there.start()
    slots[e] = x_ref[...]
    for there in copies:
        there.wait()
    total = slots[0]
    for i in range(1, ens):
        total = total + slots[i]
    out_ref[...] = total


def total_over_ens(rows):
    ens = lax.axis_size("ens")
    vmem = pl.BlockSpec(memory_space=pltpu.VMEM)
    return pl.pallas_call(
        functools.partial(small_kernel, ens),
        out_shape=jax.ShapeDtypeStruct(rows.shape, F32),
        in_specs=[vmem],
        out_specs=vmem,
        scratch_shapes=[
            pltpu.VMEM((ens,) + rows.shape, F32),
            pltpu.SemaphoreType.DMA((ens,)),
            pltpu.SemaphoreType.DMA((ens,)),
        ],
        compiler_params=pltpu.CompilerParams(collective_id=1, has_side_effects=True),
        name="small",
    )(rows)


def shards(
    embed, counts, member, bins, masses,
    gain_attn, w_qkv, w_out, pair_table, gain_ffn, w_up, w_down, w_phi, w_mean, w_scale,
):
    jets_n, slots, width = embed.shape[1:]
    heads = pair_table.shape[2]
    levels_n = pair_table.shape[1]
    ffn = w_up.shape[2]
    lengths = counts[0]
    pair_bins = bins[0]
    group_masses = masses[0]
    groups_total = group_masses.shape[0]
    steps = jets_n // TOGETHER
    block = TOGETHER * slots
    x = embed[0].reshape(jets_n * slots, width)
    weights = (gain_attn, w_qkv[0], w_out[0], gain_ffn, w_up[0], w_down[0])
    weight_specs = [whole_block(w.shape) for w in weights]
    smem = pl.BlockSpec(memory_space=pltpu.SMEM)
    params = pltpu.CompilerParams(
        dimension_semantics=("arbitrary",), vmem_limit_bytes=50 * 1024 * 1024
    )
    bins_spec = row_block((TOGETHER, slots, slots))
    kept_specs = [
        row_block((block, 3 * width)),
        row_block((TOGETHER, slots, heads * slots)),
        row_block((block, width)),
        row_block((block, width)),
    ]
    proj, att, ctx, mid, pooled_sum = pl.pallas_call(
        forward_kernel,
        grid=(steps,),
        in_specs=[smem, smem, row_block((block, width)), bins_spec] + weight_specs,
        out_specs=kept_specs + [row_block((1, TOGETHER, width))],
        out_shape=[
            jax.ShapeDtypeStruct((jets_n * slots, 3 * width), BF16),
            jax.ShapeDtypeStruct((jets_n, slots, heads * slots), BF16),
            jax.ShapeDtypeStruct((jets_n * slots, width), BF16),
            jax.ShapeDtypeStruct((jets_n * slots, width), F32),
            jax.ShapeDtypeStruct((steps, TOGETHER, width), F32),
        ],
        compiler_params=params,
        name="forward",
    )(lengths, pair_table[0], x, pair_bins, *weights)

    inverse_length = lengths[:, None].astype(F32)
    pooled = (pooled_sum.reshape(jets_n, width) / inverse_length).astype(BF16)

    def phi_part(pooled_in, w_in):
        return jax.nn.gelu(jnp.dot(pooled_in, w_in, preferred_element_type=F32))

    phi, back_phi = jax.vjp(phi_part, pooled, w_phi)
    group_onehot = (member[0][:, None] == jnp.arange(groups_total, dtype=jnp.int32)).astype(F32)
    partial_sum = jnp.dot(group_onehot.T, phi, precision=lax.Precision.HIGHEST)
    tally = jnp.sum(group_onehot, axis=0)
    joined = jnp.concatenate(
        [partial_sum, jnp.broadcast_to(tally[:, None], (groups_total, 128))], axis=1
    )
    joined = jnp.concatenate([joined, jnp.zeros((-groups_total % 8, joined.shape[1]), F32)], axis=0)
    joined = total_over_ens(joined)[:groups_total]
    summed, number = joined[:, :width], joined[:, width]

    def head_part(head_weights, summed_in):
        return flow_head(head_weights, summed_in, number, group_masses)

    neg_loglik, back_head = jax.vjp(head_part, (w_mean, w_scale), summed)
    scale_total = 1.0 / (lax.axis_size("dp") * groups_total)
    head_grads, summed_grad = back_head(jnp.full(neg_loglik.shape, scale_total, F32))
    phi_grad = jnp.dot(group_onehot, summed_grad, precision=lax.Precision.HIGHEST)
    d_pooled, d_phi = back_phi(phi_grad)
    d_pooled = (d_pooled.astype(F32) / inverse_length).reshape(steps, TOGETHER, width)
    share = 1.0 / lax.axis_size("ens")
    tail = jnp.concatenate(
        [
            d_phi.astype(F32),
            head_grads[0][None] * share,
            head_grads[1][None] * share,
            jnp.zeros((6, width), F32),
        ],
        axis=0,
    )

    base_tail = 3 * width + width + 2 * ffn + width
    unit = 8 * lax.axis_size("dp") * lax.axis_size("ens")
    used = base_tail + 8 + levels_n * heads
    flat_rows = (used + unit - 1) // unit * unit
    flat = pl.pallas_call(
        backward_kernel,
        grid=(steps,),
        in_specs=[smem, row_block((block, width)), bins_spec]
        + kept_specs
        + [row_block((1, TOGETHER, width)), whole_block(tail.shape)]
        + weight_specs,
        out_specs=whole_block((flat_rows, width)),
        out_shape=jax.ShapeDtypeStruct((flat_rows, width), F32),
        scratch_shapes=[pltpu.VMEM((levels_n * heads * 8, slots), F32)],
        compiler_params=params,
        name="backward",
    )(lengths, x, pair_bins, proj, att, ctx, mid, d_pooled, tail, *weights)

    total = total_over_all(flat)
    g_qkv = jnp.concatenate([total[i * width : (i + 1) * width] for i in range(3)], axis=1)
    at = 3 * width
    g_out = total[at : at + width]
    at += width
    g_up = jnp.concatenate(
        [total[at + i : at + i + width] for i in range(0, ffn, width)], axis=1
    )
    at += ffn
    g_down = total[at : at + ffn]
    at += ffn
    g_phi = total[at : at + width]
    small = total[base_tail : base_tail + 8 + levels_n * heads]
    g_table = jnp.sum(small[8:, :slots], axis=1).reshape(1, levels_n, heads)
    return (
        neg_loglik[None, :],
        small[0:1],
        g_qkv[None],
        g_out[None],
        g_table,
        small[1:2],
        g_up[None],
        g_down[None],
        g_phi,
        small[2],
        small[3],
    )


def solution(mesh):
    in_specs = (
        P("dp", "ens", None, None),
        P("dp", "ens"),
        P("dp", "ens"),
        P("dp", "ens", None, None),
        P("dp", None),
    ) + (P(),) * 10
    out_specs = (P("dp", None),) + (P(),) * 10
    return jax.shard_map(shards, mesh=mesh, in_specs=in_specs, out_specs=out_specs, check_vma=False)
```

```python
import functools
import math

import jax
import jax.numpy as jnp
from jax import lax
from jax.experimental import pallas as pl
from jax.experimental.pallas import tpu as pltpu
from jax.sharding import PartitionSpec as P

F32 = jnp.float32
BF16 = jnp.bfloat16
TOGETHER = 2
GELU_A = math.sqrt(2.0 / math.pi)
GELU_B = 0.044715


def dot(a, b, ca=1, cb=0):
    return lax.dot_general(a, b, (((ca,), (cb,)), ((), ())), preferred_element_type=F32)


def center(rows):
    average = jnp.mean(rows, axis=-1, keepdims=True)
    centred = rows - average
    variance = jnp.mean(centred * centred, axis=-1, keepdims=True)
    inverse = lax.rsqrt(variance + 1e-05)
    return centred * inverse, inverse


def center_back(d_hat, hat, inverse):
    first = jnp.mean(d_hat, axis=-1, keepdims=True)
    second = jnp.mean(d_hat * hat, axis=-1, keepdims=True)
    return inverse * (d_hat - first - hat * second)


def gelu_tanh(u):
    return jnp.tanh(GELU_A * (u + GELU_B * (u * u * u)))


def head_lanes(slots, width, heads):
    head_of = lax.broadcasted_iota(jnp.int32, (slots, width), 1) // (width // heads)
    return [head_of == h for h in range(heads)]


def spread(rows, lanes):
    return jnp.concatenate([rows * m.astype(F32).astype(BF16) for m in lanes], axis=0)


def collect(stacked, lanes, slots):
    out = stacked[0:slots]
    for h in range(1, len(lanes)):
        out = jnp.where(lanes[h], stacked[h * slots : (h + 1) * slots], out)
    return out


def forward_kernel(
    counts, table, x_ref, bins_ref, g1, w_qkv, w_out, g2, w_up, w_down,
    proj_o, att_o, ctx_o, mid_o, pooled_o,
):
    step = pl.program_id(0)
    slots = bins_ref.shape[1]
    width = x_ref.shape[1]
    heads = table.shape[1]
    scale = 1.0 / math.sqrt(width // heads)
    lanes = head_lanes(slots, width, heads)
    x = x_ref[...].astype(F32)
    hat, _ = center(x)
    normed = (hat * g1[...]).astype(BF16)
    proj = dot(normed, w_qkv[...]).astype(BF16)
    proj_o[...] = proj
    for j in range(TOGETHER):
        length = counts[step * TOGETHER + j]
        rows = slice(j * slots, (j + 1) * slots)
        queries = spread(proj[rows, 0:width], lanes)
        keys = proj[rows, width : 2 * width]
        values = proj[rows, 2 * width : 3 * width]
        raw = dot(keys, queries, 1, 1)
        levels = bins_ref[j].T
        bit0 = (levels & 1) == 1
        bit1 = (levels & 2) == 2
        bit2 = (levels & 4) == 4
        live = lax.broadcasted_iota(jnp.int32, (slots, slots), 0) < length
        pieces = []
        for h in range(heads):
            pair = [jnp.where(bit0, table[2 * i + 1, h], table[2 * i, h]) for i in range(4)]
            low = jnp.where(bit1, pair[1], pair[0])
            high = jnp.where(bit1, pair[3], pair[2])
            bias = jnp.where(bit2, high, low)
            score = raw[:, h * slots : (h + 1) * slots] * scale + bias
            score = jnp.where(live, score, -1e30)
            top = jnp.max(score, axis=0, keepdims=True)
            power = jnp.exp(score - top)
            total = jnp.sum(power, axis=0, keepdims=True)
            pieces.append((power * (1.0 / total)).astype(BF16))
        attend = jnp.concatenate(pieces, axis=1)
        att_o[j] = attend
        context = collect(dot(attend, values, 0, 0), lanes, slots)
        ctx_o[rows, :] = context.astype(BF16)
    middle = x + dot(ctx_o[...], w_out[...])
    mid_o[...] = middle
    hat, _ = center(middle)
    normed = (hat * g2[...]).astype(BF16)
    u = dot(normed, w_up[...])
    hidden = (0.5 * u * (1.0 + gelu_tanh(u))).astype(BF16)
    stream = (middle + dot(hidden, w_down[...])).astype(BF16).astype(F32)
    for j in range(TOGETHER):
        length = counts[step * TOGETHER + j]
        live = lax.broadcasted_iota(jnp.int32, (slots, width), 0) < length
        kept = jnp.where(live, stream[j * slots : (j + 1) * slots], 0.0)
        pooled_o[0, j : j + 1, :] = jnp.sum(kept, axis=0, keepdims=True)


def backward_kernel(
    counts, x_ref, bins_ref, proj_ref, att_ref, ctx_ref, mid_ref, back_ref, tail_ref,
    g1, w_qkv, w_out, g2, w_up, w_down,
    flat_o, table_acc,
):
    step = pl.program_id(0)
    slots = bins_ref.shape[1]
    width = x_ref.shape[1]
    ffn = w_up.shape[1]
    heads = att_ref.shape[2] // slots
    levels_n = table_acc.shape[0] // (8 * heads)
    scale = 1.0 / math.sqrt(width // heads)
    lanes = head_lanes(slots, width, heads)
    base_out = 3 * width
    base_up = base_out + width
    base_down = base_up + ffn
    base_phi = base_down + ffn
    base_tail = base_phi + width

    @pl.when(step == 0)
    def _():
        flat_o[...] = jnp.zeros(flat_o.shape, F32)
        table_acc[...] = jnp.zeros(table_acc.shape, F32)

    parts = []
    for j in range(TOGETHER):
        length = counts[step * TOGETHER + j]
        live = lax.broadcasted_iota(jnp.int32, (slots, width), 0) < length
        parts.append(jnp.where(live, back_ref[0, j : j + 1, :], 0.0))
    d_stream = jnp.concatenate(parts, axis=0)
    d_stream_b = d_stream.astype(BF16)
    middle = mid_ref[...]
    hat2, inverse2 = center(middle)
    normed2 = (hat2 * g2[...]).astype(BF16)
    d_normed = jnp.zeros(middle.shape, F32)
    for c in range(0, ffn, width):
        cols = slice(c, c + width)
        u = dot(normed2, w_up[:, cols])
        t = gelu_tanh(u)
        hidden = (0.5 * u * (1.0 + t)).astype(BF16)
        d_hidden = dot(d_stream_b, w_down[cols, :], 1, 1).astype(BF16).astype(F32)
        slope = 0.5 * (1.0 + t) + 0.5 * u * (1.0 - t * t) * (
            GELU_A * (1.0 + 3.0 * GELU_B * (u * u))
        )
        d_u = (d_hidden * slope).astype(BF16)
        flat_o[base_down + c : base_down + c + width, :] += dot(hidden, d_stream_b, 0, 0)
        flat_o[base_up + c : base_up + c + width, :] += dot(normed2, d_u, 0, 0)
        d_normed = d_normed + dot(d_u, w_up[:, cols], 1, 1)
    d_normed = d_normed.astype(BF16).astype(F32)
    flat_o[base_tail + 1 : base_tail + 2, :] += jnp.sum(d_normed * hat2, axis=0, keepdims=True)
    d_middle = d_stream_b.astype(F32) + center_back(d_normed * g2[...], hat2, inverse2)
    d_middle_b = d_middle.astype(BF16)
    d_context = dot(d_middle_b, w_out[...], 1, 1).astype(BF16)
    flat_o[base_out : base_out + width, :] += dot(ctx_ref[...], d_middle_b, 0, 0)

    d_rows = []
    for j in range(TOGETHER):
        rows = slice(j * slots, (j + 1) * slots)
        queries = spread(proj_ref[rows, 0:width], lanes)
        keys = proj_ref[rows, width : 2 * width]
        values = proj_ref[rows, 2 * width : 3 * width]
        d_ctx = spread(d_context[rows], lanes)
        attend = att_ref[j]
        d_att = dot(values, d_ctx, 1, 1)
        d_values = dot(attend, d_ctx)
        levels = bins_ref[j].T
        pieces = []
        for h in range(heads):
            cols = slice(h * slots, (h + 1) * slots)
            a = attend[:, cols].astype(F32)
            d_a = d_att[:, cols]
            inner = jnp.sum(a * d_a, axis=0, keepdims=True)
            d_s = a * (d_a - inner)
            for b in range(levels_n):
                held = jnp.where(levels == b, d_s, 0.0)
                at = (b * heads + h) * 8
                table_acc[at : at + 8, :] += jnp.sum(held.reshape(slots // 8, 8, slots), axis=0)
            pieces.append((d_s * scale).astype(BF16))
        d_score = jnp.concatenate(pieces, axis=1)
        d_keys = dot(d_score, queries)
        d_queries = collect(dot(d_score, keys, 0, 0), lanes, slots)
        d_rows.append(
            jnp.concatenate(
                [d_queries.astype(BF16), d_keys.astype(BF16), d_values.astype(BF16)], axis=1
            )
        )
    d_proj = jnp.concatenate(d_rows, axis=0)
    hat1, _ = center(x_ref[...].astype(F32))
    normed1 = (hat1 * g1[...]).astype(BF16)
    for c in range(3):
        cols = slice(c * width, (c + 1) * width)
        flat_o[c * width : (c + 1) * width, :] += dot(normed1, d_proj[:, cols], 0, 0)
    d_first = dot(d_proj, w_qkv[...], 1, 1).astype(BF16).astype(F32)
    flat_o[base_tail : base_tail + 1, :] += jnp.sum(d_first * hat1, axis=0, keepdims=True)

    @pl.when(step == pl.num_programs(0) - 1)
    def _():
        flat_o[0:base_phi, :] = flat_o[0:base_phi, :].astype(BF16).astype(F32)
        flat_o[base_phi:base_tail, :] = tail_ref[0:width, :]
        flat_o[base_tail + 2 : base_tail + 4, :] = tail_ref[width : width + 2, :]
        count = levels_n * heads
        flat_o[base_tail + 8 : base_tail + 8 + count, 0:slots] = jnp.sum(
            table_acc[...].reshape(count, 8, slots), axis=1
        )


def whole_block(shape):
    return pl.BlockSpec(shape, lambda i: (0,) * len(shape))


def row_block(shape):
    return pl.BlockSpec(shape, lambda i: (i,) + (0,) * (len(shape) - 1))


def flow_head(head_weights, summed, number, masses):
    w_mean, w_scale = head_weights
    average = summed / number[..., None]
    centre = jnp.sum(average * w_mean, axis=-1)
    log_width = jnp.sum(average * w_scale, axis=-1)
    return 0.5 * jnp.square((masses - centre) * jnp.exp(-log_width)) + log_width


MESH = pl.DeviceIdType.MESH


def greet(partners):
    barrier = pltpu.get_barrier_semaphore()
    for partner in partners:
        pl.semaphore_signal(barrier, inc=1, device_id=partner, device_id_type=MESH)
    pl.semaphore_wait(barrier, len(partners))


def reduce_kernel(ens, x_ref, out_ref, work, full, in_a, in_b, in_c, in_d, send, recv, own):
    d, e = lax.axis_index("dp"), lax.axis_index("ens")
    core, xb = d % 2, d // 2
    yb, z = e % 2, e // 2
    line = ens // 2
    half = x_ref.shape[0] // 2
    size_a, size_b, size_c = half // 2, half // 4, half // 8
    size_d = size_c // line
    count = 2 * line + 4

    def span(start, size):
        return pl.ds(pl.multiple_of(start, 8), size)

    bit_b = (1 - core) * xb + core * yb
    bit_c = (1 - core) * yb + core * xb
    step_x = 2 * (1 - 2 * xb)
    step_y = 1 - 2 * yb
    mate_a = (d + 1 - 2 * core, e)
    mate_b = (d + (1 - core) * step_x, e + core * step_y)
    mate_c = (d + core * step_x, e + (1 - core) * step_y)
    mates_d = [(d, (z + k) % line * 2 + yb) for k in range(1, line)]
    greet([mate_a, mate_b, mate_c] + mates_d)

    def copy(source, target, number, mate):
        return pltpu.make_async_remote_copy(
            src_ref=source, dst_ref=target, send_sem=send.at[number], recv_sem=recv.at[number],
            device_id=mate, device_id_type=MESH,
        )

    def one(stream):
        start_a = stream * half + core * size_a
        start_b = start_a + bit_b * size_b
        start_c = start_b + bit_c * size_c
        start_d = start_c + z * size_d

        there = copy(x_ref.at[span(stream * half + (1 - core) * size_a, size_a)], in_a.at[stream], stream * count + 0, mate_a)
        there.start()
        yield
        there.wait()
        part = span(start_a, size_a)
        work[part, :] = x_ref[part, :] + in_a[stream]

        there = copy(work.at[span(start_a + (1 - bit_b) * size_b, size_b)], in_b.at[stream], stream * count + 1, mate_b)
        there.start()
        yield
        there.wait()
        part = span(start_b, size_b)
        work[part, :] = work[part, :] + in_b[stream]

        there = copy(work.at[span(start_b + (1 - bit_c) * size_c, size_c)], in_c.at[stream], stream * count + 2, mate_c)
        there.start()
        yield
        there.wait()
        part = span(start_c, size_c)
        work[part, :] = work[part, :] + in_c[stream]

        group = []
        for k in range(1, line):
            piece = span(start_c + (z + k) % line * size_d, size_d)
            group.append(copy(work.at[piece], in_d.at[stream, k - 1], stream * count + 2 + k, mates_d[k - 1]))
        for there in group:
            there.start()
        yield
        for there in group:
            there.wait()
        part = span(start_d, size_d)
        total = work[part, :]
        for k in range(1, line):
            total = total + in_d[stream, k - 1]
        full[part, :] = total

        group = [
            copy(full.at[part], full.at[part], stream * count + 1 + line + k, mates_d[k - 1]) for k in range(1, line)
        ]
        for there in group:
            there.start()
        yield
        for there in group:
            there.wait()
        last = stream * count + 2 * line + 1
        for number, start, size, mate in (
            (last, start_c, size_c, mate_c),
            (last + 1, start_b, size_b, mate_b),
            (last + 2, start_a, size_a, mate_a),
        ):
            part = span(start, size)
            there = copy(full.at[part], full.at[part], number, mate)
            there.start()
            yield
            there.wait()

    first, second = one(0), one(1)
    next(first)
    for _ in first:
        next(second)
    for _ in second:
        pass
    back = pltpu.make_async_copy(full, out_ref, own)
    back.start()
    back.wait()


def total_over_all(flat):
    ens = lax.axis_size("ens")
    rows, width = flat.shape
    line = ens // 2
    count = 2 * (2 * line + 4)
    return pl.pallas_call(
        functools.partial(reduce_kernel, ens),
        out_shape=jax.ShapeDtypeStruct(flat.shape, F32),
        in_specs=[pl.BlockSpec(memory_space=pltpu.VMEM)],
        out_specs=pl.BlockSpec(memory_space=pl.ANY),
        scratch_shapes=[
            pltpu.VMEM((rows, width), F32),
            pltpu.VMEM((rows, width), F32),
            pltpu.VMEM((2, rows // 4, width), F32),
            pltpu.VMEM((2, rows // 8, width), F32),
            pltpu.VMEM((2, rows // 16, width), F32),
            pltpu.VMEM((2, line - 1, rows // 16 // line, width), F32),
            pltpu.SemaphoreType.DMA((count,)),
            pltpu.SemaphoreType.DMA((count,)),
            pltpu.SemaphoreType.DMA,
        ],
        compiler_params=pltpu.CompilerParams(
            collective_id=0, has_side_effects=True, vmem_limit_bytes=40 * 1024 * 1024
        ),
        name="reduce",
    )(flat)


def small_kernel(ens, x_ref, out_ref, slots, send, recv):
    d, e = lax.axis_index("dp"), lax.axis_index("ens")
    mates = [(d, (e + k) % ens) for k in range(1, ens)]
    greet(mates)
    copies = []
    for k in range(1, ens):
        copies.append(
            pltpu.make_async_remote_copy(
                src_ref=x_ref, dst_ref=slots.at[e], send_sem=send.at[k], recv_sem=recv.at[k],
                device_id=mates[k - 1], device_id_type=MESH,
            )
        )
    for there in copies:
        there.start()
    slots[e] = x_ref[...]
    for there in copies:
        there.wait()
    total = slots[0]
    for i in range(1, ens):
        total = total + slots[i]
    out_ref[...] = total


def total_over_ens(rows):
    ens = lax.axis_size("ens")
    vmem = pl.BlockSpec(memory_space=pltpu.VMEM)
    return pl.pallas_call(
        functools.partial(small_kernel, ens),
        out_shape=jax.ShapeDtypeStruct(rows.shape, F32),
        in_specs=[vmem],
        out_specs=vmem,
        scratch_shapes=[
            pltpu.VMEM((ens,) + rows.shape, F32),
            pltpu.SemaphoreType.DMA((ens,)),
            pltpu.SemaphoreType.DMA((ens,)),
        ],
        compiler_params=pltpu.CompilerParams(collective_id=1, has_side_effects=True),
        name="small",
    )(rows)


def shards(
    embed, counts, member, bins, masses,
    gain_attn, w_qkv, w_out, pair_table, gain_ffn, w_up, w_down, w_phi, w_mean, w_scale,
):
    jets_n, slots, width = embed.shape[1:]
    heads = pair_table.shape[2]
    levels_n = pair_table.shape[1]
    ffn = w_up.shape[2]
    lengths = counts[0]
    pair_bins = bins[0]
    group_masses = masses[0]
    groups_total = group_masses.shape[0]
    steps = jets_n // TOGETHER
    block = TOGETHER * slots
    x = embed[0].reshape(jets_n * slots, width)
    weights = (gain_attn, w_qkv[0], w_out[0], gain_ffn, w_up[0], w_down[0])
    weight_specs = [whole_block(w.shape) for w in weights]
    smem = pl.BlockSpec(memory_space=pltpu.SMEM)
    params = pltpu.CompilerParams(
        dimension_semantics=("arbitrary",), vmem_limit_bytes=50 * 1024 * 1024
    )
    bins_spec = row_block((TOGETHER, slots, slots))
    kept_specs = [
        row_block((block, 3 * width)),
        row_block((TOGETHER, slots, heads * slots)),
        row_block((block, width)),
        row_block((block, width)),
    ]
    proj, att, ctx, mid, pooled_sum = pl.pallas_call(
        forward_kernel,
        grid=(steps,),
        in_specs=[smem, smem, row_block((block, width)), bins_spec] + weight_specs,
        out_specs=kept_specs + [row_block((1, TOGETHER, width))],
        out_shape=[
            jax.ShapeDtypeStruct((jets_n * slots, 3 * width), BF16),
            jax.ShapeDtypeStruct((jets_n, slots, heads * slots), BF16),
            jax.ShapeDtypeStruct((jets_n * slots, width), BF16),
            jax.ShapeDtypeStruct((jets_n * slots, width), F32),
            jax.ShapeDtypeStruct((steps, TOGETHER, width), F32),
        ],
        compiler_params=params,
        name="forward",
    )(lengths, pair_table[0], x, pair_bins, *weights)

    inverse_length = lengths[:, None].astype(F32)
    pooled = (pooled_sum.reshape(jets_n, width) / inverse_length).astype(BF16)

    def phi_part(pooled_in, w_in):
        return jax.nn.gelu(jnp.dot(pooled_in, w_in, preferred_element_type=F32))

    phi, back_phi = jax.vjp(phi_part, pooled, w_phi)
    group_onehot = (member[0][:, None] == jnp.arange(groups_total, dtype=jnp.int32)).astype(F32)
    partial_sum = jnp.dot(group_onehot.T, phi, precision=lax.Precision.HIGHEST)
    tally = jnp.sum(group_onehot, axis=0)
    joined = jnp.concatenate(
        [partial_sum, jnp.broadcast_to(tally[:, None], (groups_total, 128))], axis=1
    )
    joined = jnp.concatenate([joined, jnp.zeros((-groups_total % 8, joined.shape[1]), F32)], axis=0)
    joined = total_over_ens(joined)[:groups_total]
    summed, number = joined[:, :width], joined[:, width]

    def head_part(head_weights, summed_in):
        return flow_head(head_weights, summed_in, number, group_masses)

    neg_loglik, back_head = jax.vjp(head_part, (w_mean, w_scale), summed)
    scale_total = 1.0 / (lax.axis_size("dp") * groups_total)
    head_grads, summed_grad = back_head(jnp.full(neg_loglik.shape, scale_total, F32))
    phi_grad = jnp.dot(group_onehot, summed_grad, precision=lax.Precision.HIGHEST)
    d_pooled, d_phi = back_phi(phi_grad)
    d_pooled = (d_pooled.astype(F32) / inverse_length).reshape(steps, TOGETHER, width)
    share = 1.0 / lax.axis_size("ens")
    tail = jnp.concatenate(
        [
            d_phi.astype(F32),
            head_grads[0][None] * share,
            head_grads[1][None] * share,
            jnp.zeros((6, width), F32),
        ],
        axis=0,
    )

    base_tail = 3 * width + width + 2 * ffn + width
    unit = 16 * lax.axis_size("dp") * lax.axis_size("ens")
    used = base_tail + 8 + levels_n * heads
    flat_rows = (used + unit - 1) // unit * unit
    flat = pl.pallas_call(
        backward_kernel,
        grid=(steps,),
        in_specs=[smem, row_block((block, width)), bins_spec]
        + kept_specs
        + [row_block((1, TOGETHER, width)), whole_block(tail.shape)]
        + weight_specs,
        out_specs=whole_block((flat_rows, width)),
        out_shape=jax.ShapeDtypeStruct((flat_rows, width), F32),
        scratch_shapes=[pltpu.VMEM((levels_n * heads * 8, slots), F32)],
        compiler_params=params,
        name="backward",
    )(lengths, x, pair_bins, proj, att, ctx, mid, d_pooled, tail, *weights)

    total = total_over_all(flat)
    g_qkv = jnp.concatenate([total[i * width : (i + 1) * width] for i in range(3)], axis=1)
    at = 3 * width
    g_out = total[at : at + width]
    at += width
    g_up = jnp.concatenate(
        [total[at + i : at + i + width] for i in range(0, ffn, width)], axis=1
    )
    at += ffn
    g_down = total[at : at + ffn]
    at += ffn
    g_phi = total[at : at + width]
    small = total[base_tail : base_tail + 8 + levels_n * heads]
    g_table = jnp.sum(small[8:, :slots], axis=1).reshape(1, levels_n, heads)
    return (
        neg_loglik[None, :],
        small[0:1],
        g_qkv[None],
        g_out[None],
        g_table,
        small[1:2],
        g_up[None],
        g_down[None],
        g_phi,
        small[2],
        small[3],
    )


def solution(mesh):
    in_specs = (
        P("dp", "ens", None, None),
        P("dp", "ens"),
        P("dp", "ens"),
        P("dp", "ens", None, None),
        P("dp", None),
    ) + (P(),) * 10
    out_specs = (P("dp", None),) + (P(),) * 10
    return jax.shard_map(shards, mesh=mesh, in_specs=in_specs, out_specs=out_specs, check_vma=False)
```
